32 devices in a mesh: seq: 4 (over y, x), exp: 8 (over z, core).
Axes of the slice: x: 2, y: 2, z: 4, core: 2. Of those that a mesh axis runs over, the one named last changes fastest.
Arguments:
- tokens: bfloat16 [16, 1024, 1152], P('exp', 'seq'), may hold values from -80 to 80
- timesteps: int32 [16], P('exp'), may hold values from 0 to 63
- modulation: bfloat16 [64, 2, 1152], replicated, may hold values from -0.5 to 0.5
- routes: int32 [8, 1024, 2, 2], P('exp', 'seq'), may hold values from 0 to 7, all different within a row; in each aligned block of 512 rows (0 to 511, 512 to 1023, ..., all dimensions but the last counted through in order) at most 129 rows name the same one
- gate_codes: int32 [16, 1024, 2], P('exp', 'seq'), may hold values from 1 to 16
- gate_weight: bfloat16 [8, 1152, 4608], P('exp', None, 'seq'), may hold values from -0.1875 to 0.1875
- up_weight: bfloat16 [8, 1152, 4608], P('exp', None, 'seq'), may hold values from -0.1875 to 0.1875
- down_weight: bfloat16 [8, 4608, 1152], P('exp', 'seq'), may hold values from -0.09375 to 0.09375
- cotangent: bfloat16 [16, 1024, 1152], P('exp', 'seq'), may hold values from -6 to 6
Outputs:
- grad_tokens: bfloat16 [16, 1024, 1152], P('exp', 'seq')
The draws below stay inside these ranges and needn't reach their ends.
Inputs may be any that keep to these rules, and one draw needn't show every extreme that they name: `routes`: among the rows of one device (entries [g, p, i, :] with p in one block of 256 patches, all i) no expert is named more than 129 times, a bound that some block reaches.
All inputs are finite; a program needn't handle non-finite values.
Results may differ from the reference program's by a relative error of at most 0.015.
Values may be sent and summed in bfloat16 or wider, within the bound.
No kernel may reach another device: no remote copies, remote signals or barrier semaphores. Data moves between devices by JAX's collectives and lax.ppermute only.
A program may use at most 192 MiB of HBM per device.

```python
import math
import jax
import jax.numpy as jnp
import numpy as np
from jax import lax

D = 1152
FF = 4608
PATCHES = 1024
TOP = 2
TBINS = 64
IMG_DEV = 2
EXPERTS = 8
IMAGES = 16
PATCH_DEV = 256
MOST = 129
CAP = 129
N_SEQ = 4
N_EXP = 8


def draw_tokens(key, part):
    base_key = jax.random.fold_in(key, 11)
    row_key = jax.random.fold_in(key, 12)
    column_key = jax.random.fold_in(key, 13)
    base = jnp.clip(jax.random.normal(base_key, (IMAGES, PATCHES, D), jnp.float32), -4.0, 4.0)
    row_scale = jnp.exp(jax.random.uniform(row_key, (IMAGES, PATCHES, 1), jnp.float32, 0.0, math.log(10.0)))
    column_scale = jnp.exp(jax.random.uniform(column_key, (1, 1, D), jnp.float32, 0.0, math.log(10.0)))
    return (base * row_scale * column_scale * 0.2).astype(jnp.bfloat16)


def plant(values, key, least, largest):
    dims = values.shape
    index_at = [jax.random.randint(jax.random.fold_in(key, axis), (), 0, dims[axis]) for axis in range(len(dims))]
    values = values.at[tuple(index_at)].set(least)
    longest = dims.index(max(dims))
    index_at[longest] = (index_at[longest] + 1) % dims[longest]
    return values.at[tuple(index_at)].set(largest)


def level_of(rng, dims, split, low, top_value):
    def one(axis_at, blocks):
        heights = jax.random.uniform(jax.random.fold_in(jax.random.fold_in(rng, 6), axis_at), (blocks,), jnp.float32, low / len(split), top_value / len(split))
        return jnp.repeat(jnp.exp(heights), dims[axis_at] // blocks).reshape((-1,) + (1,) * (len(dims) - axis_at - 1))

    gain = one(*split[0])
    for cut in split[1:]:
        gain = gain * one(*cut)
    return gain


def deal_out(key, own, number, rows, number_of, top, limit, skew):
    ranking = jax.random.permutation(key, number_of)
    heavy_load, common = load_shares(number_of, rows * top, limit, skew, True), load_shares(number_of, rows * top, limit, skew, False)
    places = jnp.arange(number_of)

    def named(lengths, offset_by):
        used = int((lengths > 0).sum())
        fixed = max(1, used // 4)
        shifted = fixed + (places - fixed + offset_by * (used - fixed)) % max(1, number_of - fixed)
        return jnp.zeros((number_of,), jnp.int32).at[ranking[jnp.where(places < fixed, places, shifted)]].set(jnp.asarray(lengths, jnp.int32))

    lengths = jnp.where(number % 4 == 0, named(heavy_load, number // 4), named(common, number - number // 4 - 1))
    mixed = jax.random.permutation(jax.random.fold_in(own, 3), number_of)
    donor, receiver = mixed[0:number_of // 2 * 2:2], mixed[1:number_of // 2 * 2:2]
    slack = jnp.minimum(lengths[donor] - 1, limit - lengths[receiver]) // 2
    slack = jnp.where((donor == ranking[0]) | (receiver == ranking[0]) | (lengths[receiver] == 0), 0, jnp.maximum(slack, 0))
    shifted = jax.random.randint(jax.random.fold_in(own, 4), (number_of // 2,), 0, 1 << 20) % (slack + 1)
    lengths = lengths.at[donor].add(-shifted).at[receiver].add(shifted)
    items = jnp.searchsorted(jnp.cumsum(lengths), jnp.arange(rows * top), side="right").astype(jnp.int32)
    grid = items.reshape(top, rows).T
    grid = grid[jax.random.permutation(jax.random.fold_in(own, 1), rows)]
    offset_by = jax.random.randint(jax.random.fold_in(own, 2), (rows, 1), 0, top)
    return jnp.take_along_axis(grid, (jnp.arange(top)[None, :] + offset_by) % top, axis=1)


def load_shares(amount, total, reach, skew, full):
    loads = [(1 << 20) // math.isqrt(standing ** skew) + 1 for standing in range(1, amount + 1)]
    largest = reach if full else min(reach, max(-(-total // amount), total * loads[0] // sum(loads)))
    least = 1 if total - largest >= amount - 1 else 0
    counts, surplus = [largest] + [least] * (amount - 1), total - largest - least * (amount - 1)
    while surplus > 0:
        candidates = [i for i in range(1, amount) if counts[i] < largest] or [i for i in range(1, amount) if counts[i] < reach]
        mass, left = sum([loads[i] for i in candidates]), surplus
        for i in candidates:
            addition = min(reach - counts[i], max(1, left * loads[i] // mass), surplus)
            counts[i] = counts[i] + addition
            surplus = surplus - addition
    return np.array(counts)


def noise(rng, shape, deviation, most, cuts=(), kind=jnp.bfloat16):
    drawn = jax.random.normal(rng, shape, jnp.float32) * deviation
    if len(cuts) > 0:
        drawn = level_of(rng, shape, cuts, -0.22, 0.18) * drawn
    return jnp.clip(drawn, min=-most, max=most).astype(kind)


def setup_inputs(seed: int = 0) -> dict:
    key_of = jax.random.split(jax.random.key(seed), 10)
    tokens = draw_tokens(jax.random.fold_in(key_of[9], 71), 0)
    timesteps = plant(jax.random.randint(key_of[1], (IMAGES,), 0, TBINS), jax.random.fold_in(key_of[1], 1), 0, TBINS - 1).astype(jnp.int32)
    modulation = jnp.clip(jax.random.uniform(key_of[2], (TBINS, 2, D), jnp.float32, -0.5, 0.5), -0.5, 0.5).astype(jnp.bfloat16)
    routes_keys = jax.random.split(jax.random.fold_in(key_of[3], 1), N_EXP * PATCHES * IMG_DEV // (IMG_DEV * PATCH_DEV))
    routes_turns = jax.random.permutation(jax.random.fold_in(key_of[3], 3), N_EXP * PATCHES * IMG_DEV // (IMG_DEV * PATCH_DEV))
    routes = jax.vmap(lambda own, number: deal_out(jax.random.fold_in(key_of[3], 2), own, number, IMG_DEV * PATCH_DEV, EXPERTS, TOP, MOST, 2))(routes_keys, routes_turns).reshape((N_EXP, PATCHES, IMG_DEV, TOP))
    gate_codes = plant(jax.random.randint(key_of[4], (IMAGES, PATCHES, TOP), 1, 17), jax.random.fold_in(key_of[4], 1), 1, 16).astype(jnp.int32)
    gate_weight = noise(key_of[5], (EXPERTS, D, FF), D ** -0.5, 0.1875, ((0, 8), (2, 4)))
    up_weight = noise(key_of[6], (EXPERTS, D, FF), D ** -0.5, 0.1875, ((0, 8), (2, 4)))
    down_weight = noise(key_of[7], (EXPERTS, FF, D), FF ** -0.5, 0.09375, ((0, 8), (1, 4)))
    cotangent = noise(key_of[8], (IMAGES, PATCHES, D), 1.0, 6.0, ((0, 8), (1, 4)))
    return dict(tokens=tokens, timesteps=timesteps, modulation=modulation, routes=routes, gate_codes=gate_codes, gate_weight=gate_weight, up_weight=up_weight, down_weight=down_weight, cotangent=cotangent)


def normalize_modulate(tokens_f, shift, scale):
    mean_square = lax.optimization_barrier(jnp.mean(tokens_f * tokens_f, axis=-1, keepdims=True))
    return tokens_f / jnp.sqrt(mean_square + 1e-06) * (1.0 + scale) + shift

def rounded(value):
    return lax.optimization_barrier(value.astype(jnp.bfloat16)).astype(jnp.float32)

def reference(tokens, timesteps, modulation, routes, gate_codes, gate_weight, up_weight, down_weight, cotangent):
    token_count = IMAGES * PATCHES
    table = modulation.astype(jnp.float32)[timesteps]
    scale = jnp.broadcast_to(table[:, None, 0, :], (IMAGES, PATCHES, D)).reshape(token_count, D)
    shift = jnp.broadcast_to(table[:, None, 1, :], (IMAGES, PATCHES, D)).reshape(token_count, D)
    tokens_f = tokens.astype(jnp.float32).reshape(token_count, D)
    pre, pullback = jax.vjp(lambda value: normalize_modulate(value, shift, scale), tokens_f)
    normed = pre.astype(jnp.bfloat16)
    codes = gate_codes.astype(jnp.float32).reshape(token_count, TOP)
    route_weight = (codes / lax.optimization_barrier(jnp.sum(codes, axis=-1, keepdims=True))).reshape(-1)
    flat_routes = jnp.transpose(routes, (0, 2, 1, 3)).reshape(-1)
    grads_out = cotangent.astype(jnp.float32).reshape(token_count, D)
    per_expert = N_SEQ * N_EXP * CAP
    block = FF // N_SEQ

    def expert_step(grad_sum, inputs):
        expert_id, gate_e, up_e, down_e = inputs
        gate_e = gate_e.astype(jnp.float32)
        up_e = up_e.astype(jnp.float32)
        down_e = down_e.astype(jnp.float32)
        sort_key = (flat_routes != expert_id).astype(jnp.int32)
        ordering = jnp.argsort(sort_key, stable=True)[:per_expert].astype(jnp.int32)
        is_valid = sort_key[ordering] == 0
        token_ids = (ordering // TOP).astype(jnp.int32)
        pair_weight = jnp.where(is_valid, route_weight[ordering], jnp.zeros((), jnp.float32))
        rows_in = jnp.where(is_valid[:, None], normed[token_ids], jnp.zeros((), jnp.bfloat16)).astype(jnp.float32)
        grads_in = rounded(pair_weight[:, None] * grads_out[token_ids])
        gate_pre = jnp.dot(rows_in, gate_e)
        up_pre = jnp.dot(rows_in, up_e)
        sigma = jax.nn.sigmoid(gate_pre)
        silu_gate = gate_pre * sigma
        grad_hidden = jnp.dot(grads_in, down_e.T)
        grad_gate_pre = rounded(grad_hidden * up_pre * sigma * (1.0 + gate_pre * (1.0 - sigma)))
        grad_up_pre = rounded(grad_hidden * silu_gate)
        back_sum = jnp.zeros((per_expert, D), jnp.float32)
        for block_id in range(N_SEQ):
            lower = block_id * block
            upper = lower + block
            back_term = jnp.dot(grad_gate_pre[:, lower:upper], gate_e[:, lower:upper].T)
            back_term = back_term + jnp.dot(grad_up_pre[:, lower:upper], up_e[:, lower:upper].T)
            back_sum = back_sum + rounded(back_term)
        route_back = rounded(back_sum)
        grad_sum = grad_sum.at[token_ids].add(jnp.where(is_valid[:, None], route_back, jnp.zeros((), jnp.float32)))
        return (grad_sum, None)
    start = jnp.zeros((token_count, D), jnp.float32)
    expert_ids = jnp.arange(EXPERTS, dtype=jnp.int32)
    grad_sum, unused = lax.scan(expert_step, start, (expert_ids, gate_weight, up_weight, down_weight))
    grad_tokens = pullback(grad_sum)[0]
    return grad_tokens.astype(jnp.bfloat16).reshape(IMAGES, PATCHES, D)
```

```python
import functools
import math

import jax
import jax.numpy as jnp
from jax import lax
from jax.experimental import pallas as pl
from jax.experimental.pallas import tpu as pltpu
from jax.sharding import PartitionSpec as P

AXES = ("seq", "exp")
NT = (((1,), (1,)), ((), ()))
F32 = jnp.float32
BF16 = jnp.bfloat16
VMEM_LIMIT = 60 * 2**20


def params():
    return pltpu.CompilerParams(vmem_limit_bytes=VMEM_LIMIT)


def inverse_rms(values):
    return 1.0 / jnp.sqrt(jnp.mean(values * values, axis=-1, keepdims=True) + 1e-06)


def send_kernel(images, patches, blocks, main, *refs):
    refs = refs[1:]
    levels = refs[:images]
    tokens_ref, cot_ref, routes_ref, codes_ref = refs[images : images + 4]
    outs = refs[images + 4 : images + 4 + blocks]
    place_ref, normed_ref = refs[images + 4 + blocks :]
    rows = images * patches
    for image in range(images):
        part = slice(image * patches, (image + 1) * patches)
        level = levels[image][0].astype(F32)
        x = tokens_ref[part, :].astype(F32)
        pre = x * inverse_rms(x) * (1.0 + level[0:1]) + level[1:2]
        normed_ref[part, :] = pre.astype(BF16)
    routes = routes_ref[...]
    codes = codes_ref[...].astype(F32)
    weights = codes / jnp.sum(codes, axis=0, keepdims=True)
    expert = lax.broadcasted_iota(jnp.int32, (blocks, rows), 0)
    hot = jnp.zeros((blocks, rows), F32)
    share = jnp.zeros((blocks, rows), F32)
    for top in range(routes.shape[0]):
        match = routes[top : top + 1] == expert
        hot = hot + jnp.where(match, 1.0, 0.0)
        share = share + jnp.where(match, weights[top : top + 1], 0.0)
    before = lax.broadcasted_iota(jnp.int32, (rows, rows), 0) < lax.broadcasted_iota(
        jnp.int32, (rows, rows), 1
    )
    earlier = jnp.dot(
        hot.astype(BF16), jnp.where(before, 1.0, 0.0).astype(BF16), preferred_element_type=F32
    )
    place = jnp.where(hot > 0.0, earlier, -1.0)
    place_ref[...] = place
    span = main + 8
    slot = lax.broadcasted_iota(jnp.int32, (span, rows), 0).astype(F32)
    for block in range(blocks):
        member = place[block : block + 1] == slot
        picked = jnp.where(member, 1.0, 0.0).astype(BF16)
        scale = jnp.sum(jnp.where(member, share[block : block + 1], 0.0), axis=1, keepdims=True)
        own = jnp.dot(picked, normed_ref[...], preferred_element_type=F32)
        grad = jnp.dot(picked, cot_ref[...], preferred_element_type=F32) * scale
        outs[block][0:main, :] = own[0:main].astype(BF16)
        outs[block][main : 2 * main, :] = grad[0:main].astype(BF16)
        outs[block][2 * main :, :] = jnp.concatenate([own[main:], grad[main:]], axis=0).astype(
            BF16
        )


def level_specs(images, width):
    return [
        pl.BlockSpec((1, 2, width), lambda i, levels, image=image: (levels[image], 0, 0))
        for image in range(images)
    ]


def whole(shape):
    return pl.BlockSpec(shape, lambda i, levels: (0,) * len(shape))


def make_blocks(timesteps, modulation, tokens, cotangent, routes, codes, images, blocks, main):
    rows, width = tokens.shape
    return pl.pallas_call(
        functools.partial(send_kernel, images, rows // images, blocks, main),
        grid_spec=pltpu.PrefetchScalarGridSpec(
            num_scalar_prefetch=1,
            grid=(1,),
            in_specs=level_specs(images, width)
            + [whole(tokens.shape), whole(cotangent.shape), whole(routes.shape), whole(codes.shape)],
            out_specs=[whole((2 * main + 16, width))] * blocks + [whole((blocks, rows))],
            scratch_shapes=[pltpu.VMEM((rows, width), BF16)],
        ),
        out_shape=[jax.ShapeDtypeStruct((2 * main + 16, width), BF16)] * blocks
        + [jax.ShapeDtypeStruct((blocks, rows), F32)],
        compiler_params=params(),
    )(timesteps, *([modulation] * images), tokens, cotangent, routes, codes)


def expert_kernel(count, sets, main, summed, *refs):
    arrived = refs[:count]
    hbm = refs[count : count + 3 * sets]
    base = refs[count + 3 * sets : count + 3 * sets + summed]
    out = refs[count + 3 * sets + summed]
    xs, gs, es, held, row_sem, weight_sem = refs[count + 3 * sets + summed + 1 :]
    row_copies = []
    for at in range(count):
        for source, target in (
            (slice(0, main), xs.at[at * main : (at + 1) * main, :]),
            (slice(main, 2 * main), gs.at[at * main : (at + 1) * main, :]),
            (slice(2 * main, 2 * main + 16), es.at[at * 16 : (at + 1) * 16, :]),
        ):
            row_copies.append(
                pltpu.make_async_copy(
                    arrived[at].at[source, :], target, row_sem.at[len(row_copies)]
                )
            )
            row_copies[-1].start()
    weight_copies = []
    for at in range(3 * sets):
        weight_copies.append(pltpu.make_async_copy(hbm[at], held[at], weight_sem.at[at]))
        weight_copies[-1].start()
    for copy in row_copies:
        copy.wait()
    extra = es[...].astype(F32)
    xs[count * main :, :] = jnp.concatenate(
        [extra[at * 16 : at * 16 + 8] for at in range(count)], axis=0
    ).astype(BF16)
    gs[count * main :, :] = jnp.concatenate(
        [extra[at * 16 + 8 : at * 16 + 16] for at in range(count)], axis=0
    ).astype(BF16)
    total = base[0][...].astype(F32) if summed else None
    for at in range(sets):
        gate_w, up_w, down_w = held[3 * at : 3 * at + 3]
        weight_copies[3 * at].wait()
        gate = jnp.dot(xs[...], gate_w[...], preferred_element_type=F32)
        weight_copies[3 * at + 1].wait()
        up = jnp.dot(xs[...], up_w[...], preferred_element_type=F32)
        weight_copies[3 * at + 2].wait()
        hidden = lax.dot_general(gs[...], down_w[...], NT, preferred_element_type=F32)
        sigma = jax.nn.sigmoid(gate)
        part = hidden * sigma
        grad_gate = (part * up * (1.0 + gate * (1.0 - sigma))).astype(BF16)
        grad_up = (part * gate).astype(BF16)
        back = lax.dot_general(grad_gate, gate_w[...], NT, preferred_element_type=F32)
        back = back + lax.dot_general(grad_up, up_w[...], NT, preferred_element_type=F32)
        total = back if total is None else total + back
    out[...] = total.astype(out.dtype)


def expert_part(arrived, weight_sets, main, base=None, dtype=BF16):
    count, sets = len(arrived), len(weight_sets)
    width, hidden = weight_sets[0][0].shape
    rows = count * (main + 8)
    anywhere = pl.BlockSpec(memory_space=pl.ANY)
    weights = [item for one in weight_sets for item in one]
    extra = [] if base is None else [base]
    flops = 10 * rows * width * hidden * sets
    return pl.pallas_call(
        functools.partial(expert_kernel, count, sets, main, len(extra)),
        in_specs=[anywhere] * (count + 3 * sets) + [pl.BlockSpec(memory_space=pltpu.VMEM)] * len(extra),
        out_specs=pl.BlockSpec(memory_space=pltpu.VMEM),
        out_shape=jax.ShapeDtypeStruct((rows, width), dtype),
        scratch_shapes=[
            pltpu.VMEM((rows, width), BF16),
            pltpu.VMEM((rows, width), BF16),
            pltpu.VMEM((16 * count, width), BF16),
            [pltpu.VMEM(item.shape, BF16) for item in weights],
            pltpu.SemaphoreType.DMA((3 * count,)),
            pltpu.SemaphoreType.DMA((3 * sets,)),
        ],
        compiler_params=params(),
        cost_estimate=pl.CostEstimate(
            flops=flops, bytes_accessed=sets * 6 * width * hidden + 6 * rows * width, transcendentals=0
        ),
    )(*arrived, *weights, *extra)


def finish_kernel(images, patches, blocks, main, *refs):
    refs = refs[1:]
    levels = refs[:images]
    tokens_ref, place_ref = refs[images : images + 2]
    backs = refs[images + 2 : images + 2 + blocks]
    out_ref = refs[images + 2 + blocks]
    rows = images * patches
    place = place_ref[...]
    if main % 128 == 0:
        slot = lax.broadcasted_iota(jnp.int32, (rows, main), 1).astype(F32)
        member = jnp.concatenate(
            [
                jnp.where(place[:, block : block + 1] == slot, 1.0, 0.0).astype(BF16)
                for block in range(blocks)
            ],
            axis=1,
        )
    else:
        lane = lax.broadcasted_iota(jnp.int32, (rows, blocks * main), 1)
        member = jnp.zeros((rows, blocks * main), F32)
        for block in range(blocks):
            slot = (lane - block * main).astype(F32)
            here = (lane >= block * main) & (lane < (block + 1) * main)
            member = jnp.where(here & (place[:, block : block + 1] == slot), 1.0, member)
        member = member.astype(BF16)
    lane = lax.broadcasted_iota(jnp.int32, (rows, 8 * blocks), 1)
    over = jnp.zeros((rows, 8 * blocks), F32)
    for block in range(blocks):
        slot = (lane - 8 * block + main).astype(F32)
        here = (lane >= 8 * block) & (lane < 8 * (block + 1))
        over = jnp.where(here & (place[:, block : block + 1] == slot), 1.0, over)
    grad = jnp.dot(
        member,
        jnp.concatenate([back[0:main, :] for back in backs], axis=0),
        preferred_element_type=F32,
    )
    tail = jnp.concatenate([back[main:, :].astype(F32) for back in backs], axis=0).astype(BF16)
    grad = grad + jnp.dot(over.astype(BF16), tail, preferred_element_type=F32)
    for image in range(images):
        part = slice(image * patches, (image + 1) * patches)
        level = levels[image][0].astype(F32)
        x = tokens_ref[part, :].astype(F32)
        scaled = grad[part] * (1.0 + level[0:1])
        inverse = inverse_rms(x)
        along = jnp.mean(scaled * x, axis=-1, keepdims=True) * (inverse * inverse)
        out_ref[part, :] = (inverse * (scaled - x * along)).astype(BF16)


def finish(timesteps, modulation, tokens, place, backs, images, main):
    rows, width = tokens.shape
    blocks = len(backs)
    return pl.pallas_call(
        functools.partial(finish_kernel, images, rows // images, blocks, main),
        grid_spec=pltpu.PrefetchScalarGridSpec(
            num_scalar_prefetch=1,
            grid=(1,),
            in_specs=level_specs(images, width)
            + [whole(tokens.shape), whole(place.shape)]
            + [whole(backs[0].shape)] * blocks,
            out_specs=whole(tokens.shape),
        ),
        out_shape=jax.ShapeDtypeStruct((rows, width), BF16),
        compiler_params=params(),
    )(timesteps, *([modulation] * images), tokens, place, *backs)


def per_device(
    tokens,
    timesteps,
    modulation,
    routes,
    gate_codes,
    gate_weight,
    up_weight,
    down_weight,
    cotangent,
):
    images, patches, width = tokens.shape
    top = routes.shape[3]
    rows = images * patches
    n_exp, n_seq = lax.axis_size("exp"), lax.axis_size("seq")
    blocks = n_exp * gate_weight.shape[0]
    capacity = top * rows // blocks + 1
    main = capacity - 1 if (capacity - 1) % 16 == 0 else -(-capacity // 16) * 16
    inner = 2 ** (int(math.log2(n_seq)) // 2)
    outer = n_seq // inner

    def swap_seq(value, shift, first):
        pairs = []
        for seq in range(n_seq):
            for exp in range(n_exp):
                along_inner = first if (exp % 2 == 0 or inner != outer) else not first
                other = seq ^ shift if along_inner else seq ^ (shift * inner)
                pairs.append((seq * n_exp + exp, other * n_exp + exp))
        return lax.ppermute(value, AXES, pairs)

    def swap_exp(value, shift):
        return lax.ppermute(value, "exp", [(at, at ^ shift) for at in range(n_exp)])

    own_weights = (gate_weight[0], up_weight[0], down_weight[0])
    weight_sets = [own_weights] + [
        tuple(swap_seq(item, shift, True) for item in own_weights) for shift in range(1, inner)
    ]

    me = lax.axis_index("exp")
    flat_tokens = tokens.reshape(rows, width)
    flat_cot = cotangent.reshape(rows, width)
    turned = jnp.transpose(routes[0] ^ me, (2, 1, 0)).reshape(top, rows)
    codes = jnp.transpose(gate_codes, (2, 0, 1)).reshape(top, rows)
    made = make_blocks(
        timesteps, modulation, flat_tokens, flat_cot, turned, codes, images, blocks, main
    )
    sends, place = made[:blocks], made[blocks]

    arrived = {0: sends[0]}
    order = [1] + list(range(blocks - 1, 1, -1))
    for shift in order:
        arrived[shift] = swap_exp(sends[shift], shift)
    groups = [(0, 1)] + [(at, at + 1) for at in range(blocks - 2, 1, -2)]
    backs = {}
    for group in groups:
        mine = [arrived[at] for at in group]
        returned = []
        for shift in range(1, outer):
            theirs = [swap_seq(item, shift, False) for item in mine]
            part = expert_part(theirs, weight_sets, main)
            returned.append(swap_seq(part, shift, False))
        total = expert_part(mine, weight_sets, main, dtype=F32)
        for item in returned:
            total = total + item.astype(F32)
        total = total.astype(BF16)
        count = len(group)
        for at, shift in enumerate(group):
            back = jnp.concatenate(
                [
                    total[at * main : (at + 1) * main],
                    total[count * main + 8 * at : count * main + 8 * at + 8],
                ],
                axis=0,
            )
            backs[shift] = swap_exp(back, shift) if shift else back
    out = finish(
        timesteps, modulation, flat_tokens, place.T, [backs[at] for at in range(blocks)], images, main
    )
    return out.reshape(images, patches, width)


def solution(mesh):
    in_specs = (
        P("exp", "seq", None),
        P("exp"),
        P(),
        P("exp", "seq", None, None),
        P("exp", "seq", None),
        P("exp", None, "seq"),
        P("exp", None, "seq"),
        P("exp", "seq", None),
        P("exp", "seq", None),
    )
    out_specs = P("exp", "seq", None)
    return jax.shard_map(
        per_device, mesh=mesh, in_specs=in_specs, out_specs=out_specs, check_vma=False
    )
```

```python
import functools
import math

import jax
import jax.numpy as jnp
from jax import lax
from jax.experimental import pallas as pl
from jax.experimental.pallas import tpu as pltpu
from jax.sharding import PartitionSpec as P

AXES = ("seq", "exp")
NT = (((1,), (1,)), ((), ()))
F32 = jnp.float32
BF16 = jnp.bfloat16
VMEM_LIMIT = 60 * 2**20
COST = 1000


def params():
    return pltpu.CompilerParams(vmem_limit_bytes=VMEM_LIMIT)


def inverse_rms(values):
    return 1.0 / jnp.sqrt(jnp.mean(values * values, axis=-1, keepdims=True) + 1e-06)


def send_kernel(images, patches, blocks, main, *refs):
    refs = refs[1:]
    levels = refs[:images]
    tokens_ref, cot_ref, routes_ref, codes_ref = refs[images : images + 4]
    outs = refs[images + 4 : images + 5 + blocks // 2]
    place_ref, normed_ref = refs[images + 5 + blocks // 2 :]
    rows = images * patches
    for image in range(images):
        part = slice(image * patches, (image + 1) * patches)
        level = levels[image][0].astype(F32)
        x = tokens_ref[part, :].astype(F32)
        pre = x * inverse_rms(x) * (1.0 + level[0:1]) + level[1:2]
        normed_ref[part, :] = pre.astype(BF16)
    routes = routes_ref[...]
    codes = codes_ref[...].astype(F32)
    weights = codes / jnp.sum(codes, axis=0, keepdims=True)
    expert = lax.broadcasted_iota(jnp.int32, (blocks, rows), 0)
    hot = jnp.zeros((blocks, rows), F32)
    share = jnp.zeros((blocks, rows), F32)
    for top in range(routes.shape[0]):
        match = routes[top : top + 1] == expert
        hot = hot + jnp.where(match, 1.0, 0.0)
        share = share + jnp.where(match, weights[top : top + 1], 0.0)
    before = lax.broadcasted_iota(jnp.int32, (rows, rows), 0) < lax.broadcasted_iota(
        jnp.int32, (rows, rows), 1
    )
    earlier = jnp.dot(
        hot.astype(BF16), jnp.where(before, 1.0, 0.0).astype(BF16), preferred_element_type=F32
    )
    place = jnp.where(hot > 0.0, earlier, -1.0)
    place_ref[...] = place
    slot = lax.broadcasted_iota(jnp.int32, (main + 8, rows), 0).astype(F32)
    span = 2 * main + 16
    for block in range(blocks):
        member = place[block : block + 1] == slot
        picked = jnp.where(member, 1.0, 0.0).astype(BF16)
        scale = jnp.sum(jnp.where(member, share[block : block + 1], 0.0), axis=1, keepdims=True)
        own = jnp.dot(picked, normed_ref[...], preferred_element_type=F32)
        grad = jnp.dot(picked, cot_ref[...], preferred_element_type=F32) * scale
        out = outs[block // 2] if block % 2 == 0 else outs[-1]
        start = 0 if block % 2 == 0 else block // 2 * span
        out[start : start + main, :] = own[0:main].astype(BF16)
        out[start + main : start + 2 * main, :] = grad[0:main].astype(BF16)
        out[start + 2 * main : start + span, :] = jnp.concatenate(
            [own[main:], grad[main:]], axis=0
        ).astype(BF16)


def level_specs(images, width):
    return [
        pl.BlockSpec((1, 2, width), lambda i, levels, image=image: (levels[image], 0, 0))
        for image in range(images)
    ]


def whole(shape):
    return pl.BlockSpec(shape, lambda i, levels: (0,) * len(shape))


def make_blocks(timesteps, modulation, tokens, cotangent, routes, codes, images, blocks, main):
    rows, width = tokens.shape
    half = blocks // 2
    shapes = [(2 * main + 16, width)] * half + [(half * (2 * main + 16), width)]
    return pl.pallas_call(
        functools.partial(send_kernel, images, rows // images, blocks, main),
        grid_spec=pltpu.PrefetchScalarGridSpec(
            num_scalar_prefetch=1,
            grid=(1,),
            in_specs=level_specs(images, width)
            + [whole(tokens.shape), whole(cotangent.shape), whole(routes.shape), whole(codes.shape)],
            out_specs=[whole(shape) for shape in shapes] + [whole((blocks, rows))],
            scratch_shapes=[pltpu.VMEM((rows, width), BF16)],
        ),
        out_shape=[jax.ShapeDtypeStruct(shape, BF16) for shape in shapes]
        + [jax.ShapeDtypeStruct((blocks, rows), F32)],
        compiler_params=params(),
    )(timesteps, *([modulation] * images), tokens, cotangent, routes, codes)


def expert_kernel(pairs, sets, main, bases, has_own, *refs):
    refs = list(refs)

    def take(count):
        taken = refs[:count]
        del refs[:count]
        return taken

    arrived = take(pairs)
    sources = take(3) if has_own else []
    for _ in range(sets - has_own):
        sources += take(3)
    base = take(bases)
    del refs[: len(refs) - 6 - pairs]
    outs = take(pairs)
    xs, gs, es, held, row_sem, weight_sem = refs
    span = 2 * main + 16
    row_copies = []
    for at in range(2 * pairs):
        start, origin = at // 2 * span + at % 2 * main, at % 2 * span
        for low, high, target in (
            (0, main, xs.at[start : start + main, :]),
            (main, 2 * main, gs.at[start : start + main, :]),
            (2 * main, span, es.at[at * 16 : (at + 1) * 16, :]),
        ):
            row_copies.append(
                pltpu.make_async_copy(
                    arrived[at // 2].at[origin + low : origin + high, :],
                    target,
                    row_sem.at[len(row_copies)],
                )
            )
            row_copies[-1].start()
    weight_copies = [
        pltpu.make_async_copy(sources[at], held[at], weight_sem.at[at]) for at in range(3 * sets)
    ]

    def ready(at):
        if at + 1 < 3 * sets:
            weight_copies[at + 1].start()
        weight_copies[at].wait()

    weight_copies[0].start()
    for copy in row_copies:
        copy.wait()
    extra = es[...].astype(F32)
    for pair in range(pairs):
        start = pair * span + 2 * main
        low = [extra[at * 16 : at * 16 + 8] for at in (2 * pair, 2 * pair + 1)]
        high = [extra[at * 16 + 8 : at * 16 + 16] for at in (2 * pair, 2 * pair + 1)]
        xs[start : start + 16, :] = jnp.concatenate(low, axis=0).astype(BF16)
        gs[start : start + 16, :] = jnp.concatenate(high, axis=0).astype(BF16)
    total = None
    if bases:
        total = jnp.concatenate([item[...].astype(F32) for item in base], axis=0)
    for at in range(sets):
        gate_w, up_w, down_w = held[3 * at : 3 * at + 3]
        ready(3 * at)
        gate = jnp.dot(xs[...], gate_w[...], preferred_element_type=F32)
        ready(3 * at + 1)
        up = jnp.dot(xs[...], up_w[...], preferred_element_type=F32)
        ready(3 * at + 2)
        hidden = lax.dot_general(gs[...], down_w[...], NT, preferred_element_type=F32)
        sigma = jax.nn.sigmoid(gate)
        part = hidden * sigma
        grad_gate = (part * up * (1.0 + gate * (1.0 - sigma))).astype(BF16)
        grad_up = (part * gate).astype(BF16)
        back = lax.dot_general(grad_gate, gate_w[...], NT, preferred_element_type=F32)
        back = back + lax.dot_general(grad_up, up_w[...], NT, preferred_element_type=F32)
        total = back if total is None else total + back
    for pair in range(pairs):
        outs[pair][...] = total[pair * span : (pair + 1) * span].astype(outs[pair].dtype)


def expert_part(pairs, own, others, main, bases=(), dtypes=None, after=()):
    count = len(pairs)
    has_own = 0 if own is None else 1
    sets = has_own + len(others)
    width = pairs[0].shape[1]
    hidden = own[0].shape[1] if has_own else others[0][0].shape[1]
    span = 2 * main + 16
    anywhere = pl.BlockSpec(memory_space=pl.ANY)
    inside = pl.BlockSpec(memory_space=pltpu.VMEM)
    weights = list(own or []) + [item for other in others for item in other]
    shapes = [(width, hidden), (width, hidden), (hidden, width)] * sets
    dtypes = dtypes or [F32] * count
    return pl.pallas_call(
        functools.partial(expert_kernel, count, sets, main, len(bases), has_own),
        in_specs=[anywhere] * (count + len(weights))
        + [inside] * len(bases)
        + [anywhere] * len(after),
        out_specs=[inside] * count,
        out_shape=[jax.ShapeDtypeStruct((span, width), dtype) for dtype in dtypes],
        scratch_shapes=[
            pltpu.VMEM((span * count, width), BF16),
            pltpu.VMEM((span * count, width), BF16),
            pltpu.VMEM((32 * count, width), BF16),
            [pltpu.VMEM(shape, BF16) for shape in shapes],
            pltpu.SemaphoreType.DMA((6 * count,)),
            pltpu.SemaphoreType.DMA((3 * sets,)),
        ],
        compiler_params=params(),
        cost_estimate=pl.CostEstimate(flops=COST, bytes_accessed=COST, transcendentals=0),
    )(*pairs, *weights, *bases, *after)


def finish_kernel(images, patches, blocks, main, *refs):
    refs = refs[1:]
    levels = refs[:images]
    tokens_ref, place_ref = refs[images : images + 2]
    backs = refs[images + 2 : images + 2 + blocks]
    out_ref = refs[images + 2 + blocks]
    rows = images * patches
    place = place_ref[...]
    if main % 128 == 0:
        slot = lax.broadcasted_iota(jnp.int32, (rows, main), 1).astype(F32)
        member = jnp.concatenate(
            [
                jnp.where(place[:, block : block + 1] == slot, 1.0, 0.0).astype(BF16)
                for block in range(blocks)
            ],
            axis=1,
        )
    else:
        lane = lax.broadcasted_iota(jnp.int32, (rows, blocks * main), 1)
        member = jnp.zeros((rows, blocks * main), F32)
        for block in range(blocks):
            slot = (lane - block * main).astype(F32)
            here = (lane >= block * main) & (lane < (block + 1) * main)
            member = jnp.where(here & (place[:, block : block + 1] == slot), 1.0, member)
        member = member.astype(BF16)
    lane = lax.broadcasted_iota(jnp.int32, (rows, 8 * blocks), 1)
    over = jnp.zeros((rows, 8 * blocks), F32)
    for block in range(blocks):
        slot = (lane - 8 * block + main).astype(F32)
        here = (lane >= 8 * block) & (lane < 8 * (block + 1))
        over = jnp.where(here & (place[:, block : block + 1] == slot), 1.0, over)
    grad = jnp.dot(
        member,
        jnp.concatenate([back[0:main, :] for back in backs], axis=0),
        preferred_element_type=F32,
    )
    tail = jnp.concatenate([back[main:, :].astype(F32) for back in backs], axis=0).astype(BF16)
    grad = grad + jnp.dot(over.astype(BF16), tail, preferred_element_type=F32)
    for image in range(images):
        part = slice(image * patches, (image + 1) * patches)
        level = levels[image][0].astype(F32)
        x = tokens_ref[part, :].astype(F32)
        scaled = grad[part] * (1.0 + level[0:1])
        inverse = inverse_rms(x)
        along = jnp.mean(scaled * x, axis=-1, keepdims=True) * (inverse * inverse)
        out_ref[part, :] = (inverse * (scaled - x * along)).astype(BF16)


def finish(timesteps, modulation, tokens, place, backs, images, main):
    rows, width = tokens.shape
    blocks = len(backs)
    return pl.pallas_call(
        functools.partial(finish_kernel, images, rows // images, blocks, main),
        grid_spec=pltpu.PrefetchScalarGridSpec(
            num_scalar_prefetch=1,
            grid=(1,),
            in_specs=level_specs(images, width)
            + [whole(tokens.shape), whole(place.shape)]
            + [whole(backs[0].shape)] * blocks,
            out_specs=whole(tokens.shape),
        ),
        out_shape=jax.ShapeDtypeStruct((rows, width), BF16),
        compiler_params=params(),
    )(timesteps, *([modulation] * images), tokens, place, *backs)


def per_device(
    tokens,
    timesteps,
    modulation,
    routes,
    gate_codes,
    gate_weight,
    up_weight,
    down_weight,
    cotangent,
):
    images, patches, width = tokens.shape
    top = routes.shape[3]
    rows = images * patches
    n_exp, n_seq = lax.axis_size("exp"), lax.axis_size("seq")
    blocks = n_exp * gate_weight.shape[0]
    capacity = top * rows // blocks + 1
    main = capacity - 1 if (capacity - 1) % 16 == 0 else -(-capacity // 16) * 16
    inner = 2 ** (int(math.log2(n_seq)) // 2)
    outer = n_seq // inner

    def other(seq, exp, shift, first):
        along_inner = first if (exp % 2 == 0 or inner != outer) else not first
        return seq ^ shift if along_inner else seq ^ (shift * inner)

    def swap_seq(value, shift, first):
        pairs = [
            (seq * n_exp + exp, other(seq, exp, shift, first) * n_exp + exp)
            for seq in range(n_seq)
            for exp in range(n_exp)
        ]
        return lax.ppermute(value, AXES, pairs)

    def swap_exp(value, shift):
        return lax.ppermute(value, "exp", [(at, at ^ shift) for at in range(n_exp)])

    me = lax.axis_index("exp")
    flat_tokens = tokens.reshape(rows, width)
    flat_cot = cotangent.reshape(rows, width)
    turned = jnp.transpose(routes[0] ^ me, (2, 1, 0)).reshape(top, rows)
    codes = jnp.transpose(gate_codes, (2, 0, 1)).reshape(top, rows)
    made = make_blocks(
        timesteps, modulation, flat_tokens, flat_cot, turned, codes, images, blocks, main
    )
    half = blocks // 2
    near, cross, place = made[:half], made[half], made[half + 1]

    def behind(value, *earlier):
        return lax.optimization_barrier((value, earlier))[0]

    own = (gate_weight[0], up_weight[0], down_weight[0])
    others = [
        tuple(swap_seq(item, shift, True) for item in own) for shift in range(1, inner)
    ]

    crossed = swap_exp(cross, 1)
    span = 2 * main + 16
    arrived = {}

    def send(at, *earlier):
        rows_at = jnp.concatenate([near[at], crossed[at * span : (at + 1) * span]], axis=0)
        if earlier:
            rows_at = behind(rows_at, *earlier)
        arrived[at] = swap_exp(rows_at, 2 * at) if at else rows_at

    if half == 4 and outer == 2:
        steps = [
            ("own", [(0, 0)], [], []),
            ("own", [(3, 0)], [], []),
            ("own", [(1, 0)], [], []),
            ("others", [(0, 0), (3, 0), (1, 0)], [], []),
            ("all", [(3, 1)], [], []),
            ("all", [(1, 1)], [], []),
            ("all", [(2, 0)], [3], []),
            ("all", [(2, 1)], [1], []),
            ("all", [(0, 1)], [2], [6, 7]),
        ]
        swap_after = {3: ["others"], 1: ["others"], 0: ["step", 4], 2: ["step", 5]}
        send_after = {1: 0}
    else:
        origins = range(outer)
        steps = [("all", [(at, origin) for origin in origins], [], []) for at in range(half)]
        swap_after = {at: [] for at in range(half)}
        send_after = {}

    rows_of, partial, parts, totals, backs, ran = {}, {}, {}, {}, {}, []

    def bring(at):
        after = swap_after[at]
        if not after:
            mine = arrived[at]
        elif after[0] == "step":
            mine = behind(arrived[at], ran[after[1]])
        else:
            mine = behind(arrived[at], *others[-1])
        for shift in range(1, outer):
            rows_of[at, shift] = swap_seq(mine, shift, False)

    def complete(at):
        total = parts[at, 0]
        for shift in range(1, outer):
            total = total + swap_seq(parts[at, shift], shift, False).astype(F32)
        totals[at] = total.astype(BF16)
        for core in range(2):
            back = jnp.concatenate(
                [
                    totals[at][core * main : (core + 1) * main],
                    totals[at][2 * main + 8 * core : 2 * main + 8 * core + 8],
                ],
                axis=0,
            )
            shift = 2 * at + core
            backs[shift] = swap_exp(back, shift) if shift else back

    for at in reversed(range(half)):
        if at not in send_after:
            send(at)
    for kind, items, ready, home in steps:
        for at in send_after:
            if at not in arrived and len(ran) > send_after[at]:
                send(at, ran[send_after[at]], others[-1][0])
        for at in arrived:
            rows_of[at, 0] = arrived[at]
        for at, origin in items:
            if (at, origin) not in rows_of:
                bring(at)
        bases = [partial[item] for item in items] if kind == "others" else []
        dtypes = [F32 if kind == "own" or item[1] == 0 else BF16 for item in items]
        results = expert_part(
            [rows_of[item] for item in items],
            None if kind == "others" else own,
            [] if kind == "own" else others,
            main,
            bases=bases,
            dtypes=dtypes,
            after=ran[-1:] + [totals[at] for at in ready] + [backs[at] for at in home],
        )
        ran.append(results[0])
        for item, result in zip(items, results):
            (partial if kind == "own" else parts)[item] = result
        for at in range(half):
            if at not in totals and all((at, origin) in parts for origin in range(outer)):
                complete(at)
    out = finish(
        timesteps, modulation, flat_tokens, place.T, [backs[at] for at in range(blocks)], images, main
    )
    return out.reshape(images, patches, width)


def solution(mesh):
    in_specs = (
        P("exp", "seq", None),
        P("exp"),
        P(),
        P("exp", "seq", None, None),
        P("exp", "seq", None),
        P("exp", None, "seq"),
        P("exp", None, "seq"),
        P("exp", "seq", None),
        P("exp", "seq", None),
    )
    out_specs = P("exp", "seq", None)
    return jax.shard_map(
        per_device, mesh=mesh, in_specs=in_specs, out_specs=out_specs, check_vma=False
    )
```

```python
import functools
import math

import jax
import jax.numpy as jnp
from jax import lax
from jax.experimental import pallas as pl
from jax.experimental.pallas import tpu as pltpu
from jax.sharding import PartitionSpec as P

AXES = ("seq", "exp")
NT = (((1,), (1,)), ((), ()))
F32 = jnp.float32
BF16 = jnp.bfloat16
VMEM_LIMIT = 60 * 2**20
COST = 1000
PER_US = 1.15e9


def params():
    return pltpu.CompilerParams(vmem_limit_bytes=VMEM_LIMIT)


def inverse_rms(values):
    return 1.0 / jnp.sqrt(jnp.mean(values * values, axis=-1, keepdims=True) + 1e-06)


def send_kernel(images, patches, blocks, main, *refs):
    refs = refs[1:]
    levels = refs[:images]
    tokens_ref, cot_ref, routes_ref, codes_ref = refs[images : images + 4]
    outs = refs[images + 4 : images + 5 + blocks // 2]
    place_ref, normed_ref = refs[images + 5 + blocks // 2 :]
    rows = images * patches
    for image in range(images):
        part = slice(image * patches, (image + 1) * patches)
        level = levels[image][0].astype(F32)
        x = tokens_ref[part, :].astype(F32)
        pre = x * inverse_rms(x) * (1.0 + level[0:1]) + level[1:2]
        normed_ref[part, :] = pre.astype(BF16)
    routes = routes_ref[...]
    codes = codes_ref[...].astype(F32)
    weights = codes / jnp.sum(codes, axis=0, keepdims=True)
    expert = lax.broadcasted_iota(jnp.int32, (blocks, rows), 0)
    hot = jnp.zeros((blocks, rows), F32)
    share = jnp.zeros((blocks, rows), F32)
    for top in range(routes.shape[0]):
        match = routes[top : top + 1] == expert
        hot = hot + jnp.where(match, 1.0, 0.0)
        share = share + jnp.where(match, weights[top : top + 1], 0.0)
    before = lax.broadcasted_iota(jnp.int32, (rows, rows), 0) < lax.broadcasted_iota(
        jnp.int32, (rows, rows), 1
    )
    earlier = jnp.dot(
        hot.astype(BF16), jnp.where(before, 1.0, 0.0).astype(BF16), preferred_element_type=F32
    )
    place = jnp.where(hot > 0.0, earlier, -1.0)
    place_ref[...] = place
    slot = lax.broadcasted_iota(jnp.int32, (main + 8, rows), 0).astype(F32)
    span = 2 * main + 16
    for block in range(blocks):
        member = place[block : block + 1] == slot
        picked = jnp.where(member, 1.0, 0.0).astype(BF16)
        scale = jnp.sum(jnp.where(member, share[block : block + 1], 0.0), axis=1, keepdims=True)
        own = jnp.dot(picked, normed_ref[...], preferred_element_type=F32)
        grad = jnp.dot(picked, cot_ref[...], preferred_element_type=F32) * scale
        out = outs[block // 2] if block % 2 == 0 else outs[-1]
        start = 0 if block % 2 == 0 else block // 2 * span
        out[start : start + main, :] = own[0:main].astype(BF16)
        out[start + main : start + 2 * main, :] = grad[0:main].astype(BF16)
        out[start + 2 * main : start + span, :] = jnp.concatenate(
            [own[main:], grad[main:]], axis=0
        ).astype(BF16)


def level_specs(images, width):
    return [
        pl.BlockSpec((1, 2, width), lambda i, levels, image=image: (levels[image], 0, 0))
        for image in range(images)
    ]


def whole(shape):
    return pl.BlockSpec(shape, lambda i, levels: (0,) * len(shape))


def make_blocks(timesteps, modulation, tokens, cotangent, routes, codes, images, blocks, main):
    rows, width = tokens.shape
    half = blocks // 2
    shapes = [(2 * main + 16, width)] * half + [(half * (2 * main + 16), width)]
    return pl.pallas_call(
        functools.partial(send_kernel, images, rows // images, blocks, main),
        grid_spec=pltpu.PrefetchScalarGridSpec(
            num_scalar_prefetch=1,
            grid=(1,),
            in_specs=level_specs(images, width)
            + [whole(tokens.shape), whole(cotangent.shape), whole(routes.shape), whole(codes.shape)],
            out_specs=[whole(shape) for shape in shapes] + [whole((blocks, rows))],
            scratch_shapes=[pltpu.VMEM((rows, width), BF16)],
        ),
        out_shape=[jax.ShapeDtypeStruct(shape, BF16) for shape in shapes]
        + [jax.ShapeDtypeStruct((blocks, rows), F32)],
        compiler_params=params(),
        cost_estimate=pl.CostEstimate(flops=int(8 * PER_US), bytes_accessed=COST, transcendentals=0),
    )(timesteps, *([modulation] * images), tokens, cotangent, routes, codes)


def expert_kernel(pairs, sets, main, bases, has_own, *refs):
    refs = list(refs)

    def take(count):
        taken = refs[:count]
        del refs[:count]
        return taken

    arrived = take(pairs)
    sources = take(3) if has_own else []
    for _ in range(sets - has_own):
        sources += take(3)
    base = take(bases)
    del refs[: len(refs) - 6 - pairs]
    outs = take(pairs)
    xs, gs, es, held, row_sem, weight_sem = refs
    span = 2 * main + 16
    row_copies = []
    for at in range(2 * pairs):
        start, origin = at // 2 * span + at % 2 * main, at % 2 * span
        for low, high, target in (
            (0, main, xs.at[start : start + main, :]),
            (main, 2 * main, gs.at[start : start + main, :]),
            (2 * main, span, es.at[at * 16 : (at + 1) * 16, :]),
        ):
            row_copies.append(
                pltpu.make_async_copy(
                    arrived[at // 2].at[origin + low : origin + high, :],
                    target,
                    row_sem.at[len(row_copies)],
                )
            )
            row_copies[-1].start()
    weight_copies = [
        pltpu.make_async_copy(sources[at], held[at], weight_sem.at[at]) for at in range(3 * sets)
    ]

    def ready(at):
        if at + 1 < 3 * sets:
            weight_copies[at + 1].start()
        weight_copies[at].wait()

    weight_copies[0].start()
    for copy in row_copies:
        copy.wait()
    extra = es[...].astype(F32)
    for pair in range(pairs):
        start = pair * span + 2 * main
        low = [extra[at * 16 : at * 16 + 8] for at in (2 * pair, 2 * pair + 1)]
        high = [extra[at * 16 + 8 : at * 16 + 16] for at in (2 * pair, 2 * pair + 1)]
        xs[start : start + 16, :] = jnp.concatenate(low, axis=0).astype(BF16)
        gs[start : start + 16, :] = jnp.concatenate(high, axis=0).astype(BF16)
    total = None
    if bases:
        total = jnp.concatenate([item[...].astype(F32) for item in base], axis=0)
    for at in range(sets):
        gate_w, up_w, down_w = held[3 * at : 3 * at + 3]
        ready(3 * at)
        gate = jnp.dot(xs[...], gate_w[...], preferred_element_type=F32)
        ready(3 * at + 1)
        up = jnp.dot(xs[...], up_w[...], preferred_element_type=F32)
        ready(3 * at + 2)
        hidden = lax.dot_general(gs[...], down_w[...], NT, preferred_element_type=F32)
        sigma = jax.nn.sigmoid(gate)
        part = hidden * sigma
        grad_gate = (part * up * (1.0 + gate * (1.0 - sigma))).astype(BF16)
        grad_up = (part * gate).astype(BF16)
        back = lax.dot_general(grad_gate, gate_w[...], NT, preferred_element_type=F32)
        back = back + lax.dot_general(grad_up, up_w[...], NT, preferred_element_type=F32)
        total = back if total is None else total + back
    for pair in range(pairs):
        outs[pair][...] = total[pair * span : (pair + 1) * span].astype(outs[pair].dtype)


def expert_part(pairs, own, others, main, bases=(), dtypes=None, after=()):
    count = len(pairs)
    has_own = 0 if own is None else 1
    sets = has_own + len(others)
    width = pairs[0].shape[1]
    hidden = own[0].shape[1] if has_own else others[0][0].shape[1]
    span = 2 * main + 16
    anywhere = pl.BlockSpec(memory_space=pl.ANY)
    inside = pl.BlockSpec(memory_space=pltpu.VMEM)
    weights = list(own or []) + [item for other in others for item in other]
    shapes = [(width, hidden), (width, hidden), (hidden, width)] * sets
    dtypes = dtypes or [F32] * count
    return pl.pallas_call(
        functools.partial(expert_kernel, count, sets, main, len(bases), has_own),
        in_specs=[anywhere] * (count + len(weights))
        + [inside] * len(bases)
        + [anywhere] * len(after),
        out_specs=[inside] * count,
        out_shape=[jax.ShapeDtypeStruct((span, width), dtype) for dtype in dtypes],
        scratch_shapes=[
            pltpu.VMEM((span * count, width), BF16),
            pltpu.VMEM((span * count, width), BF16),
            pltpu.VMEM((32 * count, width), BF16),
            [pltpu.VMEM(shape, BF16) for shape in shapes],
            pltpu.SemaphoreType.DMA((6 * count,)),
            pltpu.SemaphoreType.DMA((3 * sets,)),
        ],
        compiler_params=params(),
        cost_estimate=pl.CostEstimate(
            flops=int((4 + 5 * count * sets) * PER_US), bytes_accessed=COST, transcendentals=0
        ),
    )(*pairs, *weights, *bases, *after)


def finish_kernel(images, patches, blocks, main, *refs):
    refs = refs[1:]
    levels = refs[:images]
    tokens_ref, place_ref = refs[images : images + 2]
    backs = refs[images + 2 : images + 2 + blocks]
    out_ref = refs[images + 2 + blocks]
    rows = images * patches
    place = place_ref[...]
    if main % 128 == 0:
        slot = lax.broadcasted_iota(jnp.int32, (rows, main), 1).astype(F32)
        member = jnp.concatenate(
            [
                jnp.where(place[:, block : block + 1] == slot, 1.0, 0.0).astype(BF16)
                for block in range(blocks)
            ],
            axis=1,
        )
    else:
        lane = lax.broadcasted_iota(jnp.int32, (rows, blocks * main), 1)
        member = jnp.zeros((rows, blocks * main), F32)
        for block in range(blocks):
            slot = (lane - block * main).astype(F32)
            here = (lane >= block * main) & (lane < (block + 1) * main)
            member = jnp.where(here & (place[:, block : block + 1] == slot), 1.0, member)
        member = member.astype(BF16)
    lane = lax.broadcasted_iota(jnp.int32, (rows, 8 * blocks), 1)
    over = jnp.zeros((rows, 8 * blocks), F32)
    for block in range(blocks):
        slot = (lane - 8 * block + main).astype(F32)
        here = (lane >= 8 * block) & (lane < 8 * (block + 1))
        over = jnp.where(here & (place[:, block : block + 1] == slot), 1.0, over)
    grad = jnp.dot(
        member,
        jnp.concatenate([back[0:main, :] for back in backs], axis=0),
        preferred_element_type=F32,
    )
    tail = jnp.concatenate([back[main:, :].astype(F32) for back in backs], axis=0).astype(BF16)
    grad = grad + jnp.dot(over.astype(BF16), tail, preferred_element_type=F32)
    for image in range(images):
        part = slice(image * patches, (image + 1) * patches)
        level = levels[image][0].astype(F32)
        x = tokens_ref[part, :].astype(F32)
        scaled = grad[part] * (1.0 + level[0:1])
        inverse = inverse_rms(x)
        along = jnp.mean(scaled * x, axis=-1, keepdims=True) * (inverse * inverse)
        out_ref[part, :] = (inverse * (scaled - x * along)).astype(BF16)


def finish(timesteps, modulation, tokens, place, backs, images, main):
    rows, width = tokens.shape
    blocks = len(backs)
    return pl.pallas_call(
        functools.partial(finish_kernel, images, rows // images, blocks, main),
        grid_spec=pltpu.PrefetchScalarGridSpec(
            num_scalar_prefetch=1,
            grid=(1,),
            in_specs=level_specs(images, width)
            + [whole(tokens.shape), whole(place.shape)]
            + [whole(backs[0].shape)] * blocks,
            out_specs=whole(tokens.shape),
        ),
        out_shape=jax.ShapeDtypeStruct((rows, width), BF16),
        compiler_params=params(),
    )(timesteps, *([modulation] * images), tokens, place, *backs)


def per_device(
    tokens,
    timesteps,
    modulation,
    routes,
    gate_codes,
    gate_weight,
    up_weight,
    down_weight,
    cotangent,
):
    images, patches, width = tokens.shape
    top = routes.shape[3]
    rows = images * patches
    n_exp, n_seq = lax.axis_size("exp"), lax.axis_size("seq")
    blocks = n_exp * gate_weight.shape[0]
    capacity = top * rows // blocks + 1
    main = capacity - 1 if (capacity - 1) % 16 == 0 else -(-capacity // 16) * 16
    inner = 2 ** (int(math.log2(n_seq)) // 2)
    outer = n_seq // inner

    def other(seq, exp, shift, first):
        along_inner = first if (exp % 2 == 0 or inner != outer) else not first
        return seq ^ shift if along_inner else seq ^ (shift * inner)

    def swap_seq(value, shift, first):
        pairs = [
            (seq * n_exp + exp, other(seq, exp, shift, first) * n_exp + exp)
            for seq in range(n_seq)
            for exp in range(n_exp)
        ]
        return lax.ppermute(value, AXES, pairs)

    def swap_exp(value, shift):
        return lax.ppermute(value, "exp", [(at, at ^ shift) for at in range(n_exp)])

    me = lax.axis_index("exp")
    flat_tokens = tokens.reshape(rows, width)
    flat_cot = cotangent.reshape(rows, width)
    turned = jnp.transpose(routes[0] ^ me, (2, 1, 0)).reshape(top, rows)
    codes = jnp.transpose(gate_codes, (2, 0, 1)).reshape(top, rows)
    made = make_blocks(
        timesteps, modulation, flat_tokens, flat_cot, turned, codes, images, blocks, main
    )
    half = blocks // 2
    near, cross, place = made[:half], made[half], made[half + 1]

    def behind(value, *earlier):
        return lax.optimization_barrier((value, earlier))[0]

    own = (gate_weight[0], up_weight[0], down_weight[0])
    others = [
        tuple(swap_seq(item, shift, True) for item in own) for shift in range(1, inner)
    ]

    crossed = swap_exp(cross, 1)
    span = 2 * main + 16
    arrived = {}

    def send(at, *earlier):
        rows_at = jnp.concatenate([near[at], crossed[at * span : (at + 1) * span]], axis=0)
        if earlier:
            rows_at = behind(rows_at, *earlier)
        arrived[at] = swap_exp(rows_at, 2 * at) if at else rows_at

    if half == 4 and outer == 2:
        steps = [
            ("own", [(0, 0)], [], []),
            ("own", [(3, 0)], [], []),
            ("own", [(1, 0)], [], []),
            ("others", [(0, 0), (3, 0), (1, 0)], [], []),
            ("all", [(0, 1)], [], []),
            ("all", [(3, 1), (2, 0)], [], []),
            ("all", [(2, 1), (1, 1)], [0], []),
        ]
        swap_after = {0: ["others", 2], 3: ["others", 2], 2: ["step", 3], 1: ["step", 4]}
        send_after = {1: 0}
        two_hops = (3,)
    else:
        origins = range(outer)
        steps = [("all", [(at, origin) for origin in origins], [], []) for at in range(half)]
        swap_after = {at: [] for at in range(half)}
        send_after = {}
        two_hops = ()

    rows_of, partial, parts, totals, backs, ran = {}, {}, {}, {}, {}, []

    def bring(at):
        after = swap_after[at]
        if not after:
            mine = arrived[at]
        elif after[0] == "step":
            mine = behind(arrived[at], ran[after[1]])
        else:
            mine = behind(arrived[at], ran[after[1]], *others[-1])
        for shift in range(1, outer):
            rows_of[at, shift] = swap_seq(mine, shift, False)

    def complete(at):
        total = parts[at, 0]
        for shift in range(1, outer):
            total = total + swap_seq(parts[at, shift], shift, False).astype(F32)
        totals[at] = total.astype(BF16)

        def block(value, core):
            return jnp.concatenate(
                [
                    value[core * main : (core + 1) * main],
                    value[2 * main + 8 * core : 2 * main + 8 * core + 8],
                ],
                axis=0,
            )

        if at in two_hops:
            home = swap_exp(totals[at], 2 * at)
            backs[2 * at] = block(home, 0)
            backs[2 * at + 1] = block(swap_exp(home, 1), 1)
            return
        for core in range(2):
            shift = 2 * at + core
            back = block(totals[at], core)
            backs[shift] = swap_exp(back, shift) if shift else back

    for at in reversed(range(half)):
        if at not in send_after:
            send(at)
    for kind, items, ready, home in steps:
        for at in send_after:
            if at not in arrived and len(ran) > send_after[at]:
                send(at, ran[send_after[at]], others[-1][0])
        for at in arrived:
            rows_of[at, 0] = arrived[at]
        for at, origin in items:
            if (at, origin) not in rows_of:
                bring(at)
        bases = [partial[item] for item in items] if kind == "others" else []
        dtypes = [F32 if kind == "own" or item[1] == 0 else BF16 for item in items]
        results = expert_part(
            [rows_of[item] for item in items],
            None if kind == "others" else own,
            [] if kind == "own" else others,
            main,
            bases=bases,
            dtypes=dtypes,
            after=ran[-1:] + [totals[at] for at in ready] + [backs[at] for at in home],
        )
        ran.append(results[0])
        for item, result in zip(items, results):
            (partial if kind == "own" else parts)[item] = result
        for at in range(half):
            if at not in totals and all((at, origin) in parts for origin in range(outer)):
                complete(at)
    out = finish(
        timesteps, modulation, flat_tokens, place.T, [backs[at] for at in range(blocks)], images, main
    )
    return out.reshape(images, patches, width)


def solution(mesh):
    in_specs = (
        P("exp", "seq", None),
        P("exp"),
        P(),
        P("exp", "seq", None, None),
        P("exp", "seq", None),
        P("exp", None, "seq"),
        P("exp", None, "seq"),
        P("exp", "seq", None),
        P("exp", "seq", None),
    )
    out_specs = P("exp", "seq", None)
    return jax.shard_map(
        per_device, mesh=mesh, in_specs=in_specs, out_specs=out_specs, check_vma=False
    )
```

```python
import functools
import math

import jax
import jax.numpy as jnp
from jax import lax
from jax.experimental import pallas as pl
from jax.experimental.pallas import tpu as pltpu
from jax.sharding import PartitionSpec as P

AXES = ("seq", "exp")
NT = (((1,), (1,)), ((), ()))
F32 = jnp.float32
BF16 = jnp.bfloat16
VMEM_LIMIT = 60 * 2**20
COST = 1000
PER_US = 1.15e9


def params():
    return pltpu.CompilerParams(vmem_limit_bytes=VMEM_LIMIT)


def inverse_rms(values):
    return 1.0 / jnp.sqrt(jnp.mean(values * values, axis=-1, keepdims=True) + 1e-06)


def send_kernel(images, patches, blocks, main, *refs):
    refs = refs[1:]
    levels = refs[:images]
    tokens_ref, cot_ref, routes_ref, codes_ref = refs[images : images + 4]
    outs = refs[images + 4 : images + 5 + blocks // 2]
    place_ref, normed_ref = refs[images + 5 + blocks // 2 :]
    rows = images * patches
    for image in range(images):
        part = slice(image * patches, (image + 1) * patches)
        level = levels[image][0].astype(F32)
        x = tokens_ref[part, :].astype(F32)
        pre = x * inverse_rms(x) * (1.0 + level[0:1]) + level[1:2]
        normed_ref[part, :] = pre.astype(BF16)
    routes = routes_ref[...]
    codes = codes_ref[...].astype(F32)
    weights = codes / jnp.sum(codes, axis=0, keepdims=True)
    expert = lax.broadcasted_iota(jnp.int32, (blocks, rows), 0)
    hot = jnp.zeros((blocks, rows), F32)
    share = jnp.zeros((blocks, rows), F32)
    for top in range(routes.shape[0]):
        match = routes[top : top + 1] == expert
        hot = hot + jnp.where(match, 1.0, 0.0)
        share = share + jnp.where(match, weights[top : top + 1], 0.0)
    before = lax.broadcasted_iota(jnp.int32, (rows, rows), 0) < lax.broadcasted_iota(
        jnp.int32, (rows, rows), 1
    )
    earlier = jnp.dot(
        hot.astype(BF16), jnp.where(before, 1.0, 0.0).astype(BF16), preferred_element_type=F32
    )
    place = jnp.where(hot > 0.0, earlier, -1.0)
    place_ref[...] = place
    slot = lax.broadcasted_iota(jnp.int32, (main + 8, rows), 0).astype(F32)
    span = 2 * main + 16
    for block in range(blocks):
        member = place[block : block + 1] == slot
        picked = jnp.where(member, 1.0, 0.0).astype(BF16)
        scale = jnp.sum(jnp.where(member, share[block : block + 1], 0.0), axis=1, keepdims=True)
        own = jnp.dot(picked, normed_ref[...], preferred_element_type=F32)
        grad = jnp.dot(picked, cot_ref[...], preferred_element_type=F32) * scale
        out = outs[block // 2] if block % 2 == 0 else outs[-1]
        start = 0 if block % 2 == 0 else block // 2 * span
        out[start : start + main, :] = own[0:main].astype(BF16)
        out[start + main : start + 2 * main, :] = grad[0:main].astype(BF16)
        out[start + 2 * main : start + span, :] = jnp.concatenate(
            [own[main:], grad[main:]], axis=0
        ).astype(BF16)


def level_specs(images, width):
    return [
        pl.BlockSpec((1, 2, width), lambda i, levels, image=image: (levels[image], 0, 0))
        for image in range(images)
    ]


def whole(shape):
    return pl.BlockSpec(shape, lambda i, levels: (0,) * len(shape))


def make_blocks(timesteps, modulation, tokens, cotangent, routes, codes, images, blocks, main):
    rows, width = tokens.shape
    half = blocks // 2
    shapes = [(2 * main + 16, width)] * half + [(half * (2 * main + 16), width)]
    return pl.pallas_call(
        functools.partial(send_kernel, images, rows // images, blocks, main),
        grid_spec=pltpu.PrefetchScalarGridSpec(
            num_scalar_prefetch=1,
            grid=(1,),
            in_specs=level_specs(images, width)
            + [whole(tokens.shape), whole(cotangent.shape), whole(routes.shape), whole(codes.shape)],
            out_specs=[whole(shape) for shape in shapes] + [whole((blocks, rows))],
            scratch_shapes=[pltpu.VMEM((rows, width), BF16)],
        ),
        out_shape=[jax.ShapeDtypeStruct(shape, BF16) for shape in shapes]
        + [jax.ShapeDtypeStruct((blocks, rows), F32)],
        compiler_params=params(),
        cost_estimate=pl.CostEstimate(flops=int(8 * PER_US), bytes_accessed=COST, transcendentals=0),
    )(timesteps, *([modulation] * images), tokens, cotangent, routes, codes)


def expert_kernel(pairs, sets, main, bases, has_own, *refs):
    refs = list(refs)

    def take(count):
        taken = refs[:count]
        del refs[:count]
        return taken

    arrived = take(pairs)
    sources = take(3) if has_own else []
    for _ in range(sets - has_own):
        sources += take(3)
    base = take(bases)
    del refs[: len(refs) - 6 - pairs]
    outs = take(pairs)
    xs, gs, es, held, row_sem, weight_sem = refs
    span = 2 * main + 16
    row_copies = []
    for at in range(2 * pairs):
        start, origin = at // 2 * span + at % 2 * main, at % 2 * span
        for low, high, target in (
            (0, main, xs.at[start : start + main, :]),
            (main, 2 * main, gs.at[start : start + main, :]),
            (2 * main, span, es.at[at * 16 : (at + 1) * 16, :]),
        ):
            row_copies.append(
                pltpu.make_async_copy(
                    arrived[at // 2].at[origin + low : origin + high, :],
                    target,
                    row_sem.at[len(row_copies)],
                )
            )
            row_copies[-1].start()
    weight_copies = [
        pltpu.make_async_copy(sources[at], held[at], weight_sem.at[at]) for at in range(3 * sets)
    ]

    def ready(at):
        if at + 1 < 3 * sets:
            weight_copies[at + 1].start()
        weight_copies[at].wait()

    weight_copies[0].start()
    for copy in row_copies:
        copy.wait()
    extra = es[...].astype(F32)
    for pair in range(pairs):
        start = pair * span + 2 * main
        low = [extra[at * 16 : at * 16 + 8] for at in (2 * pair, 2 * pair + 1)]
        high = [extra[at * 16 + 8 : at * 16 + 16] for at in (2 * pair, 2 * pair + 1)]
        xs[start : start + 16, :] = jnp.concatenate(low, axis=0).astype(BF16)
        gs[start : start + 16, :] = jnp.concatenate(high, axis=0).astype(BF16)
    total = None
    if bases:
        total = jnp.concatenate([item[...].astype(F32) for item in base], axis=0)
    for at in range(sets):
        gate_w, up_w, down_w = held[3 * at : 3 * at + 3]
        ready(3 * at)
        gate = jnp.dot(xs[...], gate_w[...], preferred_element_type=F32)
        ready(3 * at + 1)
        up = jnp.dot(xs[...], up_w[...], preferred_element_type=F32)
        ready(3 * at + 2)
        hidden = lax.dot_general(gs[...], down_w[...], NT, preferred_element_type=F32)
        sigma = jax.nn.sigmoid(gate)
        part = hidden * sigma
        grad_gate = (part * up * (1.0 + gate * (1.0 - sigma))).astype(BF16)
        grad_up = (part * gate).astype(BF16)
        back = lax.dot_general(grad_gate, gate_w[...], NT, preferred_element_type=F32)
        back = back + lax.dot_general(grad_up, up_w[...], NT, preferred_element_type=F32)
        total = back if total is None else total + back
    for pair in range(pairs):
        outs[pair][...] = total[pair * span : (pair + 1) * span].astype(outs[pair].dtype)


def expert_part(pairs, own, others, main, bases=(), dtypes=None, after=()):
    count = len(pairs)
    has_own = 0 if own is None else 1
    sets = has_own + len(others)
    width = pairs[0].shape[1]
    hidden = own[0].shape[1] if has_own else others[0][0].shape[1]
    span = 2 * main + 16
    anywhere = pl.BlockSpec(memory_space=pl.ANY)
    inside = pl.BlockSpec(memory_space=pltpu.VMEM)
    weights = list(own or []) + [item for other in others for item in other]
    shapes = [(width, hidden), (width, hidden), (hidden, width)] * sets
    dtypes = dtypes or [F32] * count
    return pl.pallas_call(
        functools.partial(expert_kernel, count, sets, main, len(bases), has_own),
        in_specs=[anywhere] * (count + len(weights))
        + [inside] * len(bases)
        + [anywhere] * len(after),
        out_specs=[inside] * count,
        out_shape=[jax.ShapeDtypeStruct((span, width), dtype) for dtype in dtypes],
        scratch_shapes=[
            pltpu.VMEM((span * count, width), BF16),
            pltpu.VMEM((span * count, width), BF16),
            pltpu.VMEM((32 * count, width), BF16),
            [pltpu.VMEM(shape, BF16) for shape in shapes],
            pltpu.SemaphoreType.DMA((6 * count,)),
            pltpu.SemaphoreType.DMA((3 * sets,)),
        ],
        compiler_params=params(),
        cost_estimate=pl.CostEstimate(
            flops=int((4 + 5 * count * sets) * PER_US), bytes_accessed=COST, transcendentals=0
        ),
    )(*pairs, *weights, *bases, *after)


def finish_kernel(images, patches, blocks, main, *refs):
    refs = refs[1:]
    levels = refs[:images]
    tokens_ref, place_ref = refs[images : images + 2]
    backs = refs[images + 2 : images + 2 + blocks]
    out_ref = refs[images + 2 + blocks]
    rows = images * patches
    place = place_ref[...]
    if main % 128 == 0:
        slot = lax.broadcasted_iota(jnp.int32, (rows, main), 1).astype(F32)
        member = jnp.concatenate(
            [
                jnp.where(place[:, block : block + 1] == slot, 1.0, 0.0).astype(BF16)
                for block in range(blocks)
            ],
            axis=1,
        )
    else:
        lane = lax.broadcasted_iota(jnp.int32, (rows, blocks * main), 1)
        member = jnp.zeros((rows, blocks * main), F32)
        for block in range(blocks):
            slot = (lane - block * main).astype(F32)
            here = (lane >= block * main) & (lane < (block + 1) * main)
            member = jnp.where(here & (place[:, block : block + 1] == slot), 1.0, member)
        member = member.astype(BF16)
    lane = lax.broadcasted_iota(jnp.int32, (rows, 8 * blocks), 1)
    over = jnp.zeros((rows, 8 * blocks), F32)
    for block in range(blocks):
        slot = (lane - 8 * block + main).astype(F32)
        here = (lane >= 8 * block) & (lane < 8 * (block + 1))
        over = jnp.where(here & (place[:, block : block + 1] == slot), 1.0, over)
    grad = jnp.dot(
        member,
        jnp.concatenate([back[0:main, :] for back in backs], axis=0),
        preferred_element_type=F32,
    )
    tail = jnp.concatenate([back[main:, :].astype(F32) for back in backs], axis=0).astype(BF16)
    grad = grad + jnp.dot(over.astype(BF16), tail, preferred_element_type=F32)
    for image in range(images):
        part = slice(image * patches, (image + 1) * patches)
        level = levels[image][0].astype(F32)
        x = tokens_ref[part, :].astype(F32)
        scaled = grad[part] * (1.0 + level[0:1])
        inverse = inverse_rms(x)
        along = jnp.mean(scaled * x, axis=-1, keepdims=True) * (inverse * inverse)
        out_ref[part, :] = (inverse * (scaled - x * along)).astype(BF16)


def finish(timesteps, modulation, tokens, place, backs, images, main):
    rows, width = tokens.shape
    blocks = len(backs)
    return pl.pallas_call(
        functools.partial(finish_kernel, images, rows // images, blocks, main),
        grid_spec=pltpu.PrefetchScalarGridSpec(
            num_scalar_prefetch=1,
            grid=(1,),
            in_specs=level_specs(images, width)
            + [whole(tokens.shape), whole(place.shape)]
            + [whole(backs[0].shape)] * blocks,
            out_specs=whole(tokens.shape),
        ),
        out_shape=jax.ShapeDtypeStruct((rows, width), BF16),
        compiler_params=params(),
    )(timesteps, *([modulation] * images), tokens, place, *backs)


def per_device(
    tokens,
    timesteps,
    modulation,
    routes,
    gate_codes,
    gate_weight,
    up_weight,
    down_weight,
    cotangent,
):
    images, patches, width = tokens.shape
    top = routes.shape[3]
    rows = images * patches
    n_exp, n_seq = lax.axis_size("exp"), lax.axis_size("seq")
    blocks = n_exp * gate_weight.shape[0]
    capacity = top * rows // blocks + 1
    main = capacity - 1 if (capacity - 1) % 16 == 0 else -(-capacity // 16) * 16
    inner = 2 ** (int(math.log2(n_seq)) // 2)
    outer = n_seq // inner

    def other(seq, exp, shift, first):
        along_inner = first if (exp % 2 == 0 or inner != outer) else not first
        return seq ^ shift if along_inner else seq ^ (shift * inner)

    def swap_seq(value, shift, first):
        pairs = [
            (seq * n_exp + exp, other(seq, exp, shift, first) * n_exp + exp)
            for seq in range(n_seq)
            for exp in range(n_exp)
        ]
        return lax.ppermute(value, AXES, pairs)

    def swap_exp(value, shift):
        return lax.ppermute(value, "exp", [(at, at ^ shift) for at in range(n_exp)])

    me = lax.axis_index("exp")
    flat_tokens = tokens.reshape(rows, width)
    flat_cot = cotangent.reshape(rows, width)
    turned = jnp.transpose(routes[0] ^ me, (2, 1, 0)).reshape(top, rows)
    codes = jnp.transpose(gate_codes, (2, 0, 1)).reshape(top, rows)
    made = make_blocks(
        timesteps, modulation, flat_tokens, flat_cot, turned, codes, images, blocks, main
    )
    half = blocks // 2
    near, cross, place = made[:half], made[half], made[half + 1]

    def behind(value, *earlier):
        return lax.optimization_barrier((value, earlier))[0]

    own = (gate_weight[0], up_weight[0], down_weight[0])
    others = [
        tuple(swap_seq(item, shift, True) for item in own) for shift in range(1, inner)
    ]

    crossed = swap_exp(cross, 1)
    span = 2 * main + 16
    arrived = {}

    def send(at, *earlier):
        rows_at = jnp.concatenate([near[at], crossed[at * span : (at + 1) * span]], axis=0)
        if earlier:
            rows_at = behind(rows_at, *earlier)
        arrived[at] = swap_exp(rows_at, 2 * at) if at else rows_at

    if half == 4 and outer == 2:
        steps = [
            ("own", [(0, 0)], [], []),
            ("own", [(3, 0)], [], []),
            ("own", [(1, 0)], [], []),
            ("others", [(0, 0), (3, 0), (1, 0)], [], []),
            ("all", [(0, 1)], [], []),
            ("all", [(3, 1), (2, 0)], [], []),
            ("all", [(2, 1), (1, 1)], [0], []),
        ]
        swap_after = {0: ["others", 2], 3: ["others", 2], 2: ["step", 3], 1: ["step", 4]}
        send_after = {1: 0}
    else:
        origins = range(outer)
        steps = [("all", [(at, origin) for origin in origins], [], []) for at in range(half)]
        swap_after = {at: [] for at in range(half)}
        send_after = {}

    rows_of, partial, parts, totals, backs, ran = {}, {}, {}, {}, {}, []

    def bring(at):
        after = swap_after[at]
        if not after:
            mine = arrived[at]
        elif after[0] == "step":
            mine = behind(arrived[at], ran[after[1]])
        else:
            mine = behind(arrived[at], ran[after[1]], *others[-1])
        for shift in range(1, outer):
            rows_of[at, shift] = swap_seq(mine, shift, False)

    def complete(at):
        total = parts[at, 0]
        for shift in range(1, outer):
            total = total + swap_seq(parts[at, shift], shift, False).astype(F32)
        totals[at] = total.astype(BF16)
        for core in range(2):
            back = jnp.concatenate(
                [
                    totals[at][core * main : (core + 1) * main],
                    totals[at][2 * main + 8 * core : 2 * main + 8 * core + 8],
                ],
                axis=0,
            )
            shift = 2 * at + core
            backs[shift] = swap_exp(back, shift) if shift else back

    for at in reversed(range(half)):
        if at not in send_after:
            send(at)
    for kind, items, ready, home in steps:
        for at in send_after:
            if at not in arrived and len(ran) > send_after[at]:
                send(at, ran[send_after[at]], others[-1][0])
        for at in arrived:
            rows_of[at, 0] = arrived[at]
        for at, origin in items:
            if (at, origin) not in rows_of:
                bring(at)
        bases = [partial[item] for item in items] if kind == "others" else []
        dtypes = [F32 if kind == "own" or item[1] == 0 else BF16 for item in items]
        results = expert_part(
            [rows_of[item] for item in items],
            None if kind == "others" else own,
            [] if kind == "own" else others,
            main,
            bases=bases,
            dtypes=dtypes,
            after=ran[-1:] + [totals[at] for at in ready] + [backs[at] for at in home],
        )
        ran.append(results[0])
        for item, result in zip(items, results):
            (partial if kind == "own" else parts)[item] = result
        for at in range(half):
            if at not in totals and all((at, origin) in parts for origin in range(outer)):
                complete(at)
    out = finish(
        timesteps, modulation, flat_tokens, place.T, [backs[at] for at in range(blocks)], images, main
    )
    return out.reshape(images, patches, width)


def solution(mesh):
    in_specs = (
        P("exp", "seq", None),
        P("exp"),
        P(),
        P("exp", "seq", None, None),
        P("exp", "seq", None),
        P("exp", None, "seq"),
        P("exp", None, "seq"),
        P("exp", "seq", None),
        P("exp", "seq", None),
    )
    out_specs = P("exp", "seq", None)
    return jax.shard_map(
        per_device, mesh=mesh, in_specs=in_specs, out_specs=out_specs, check_vma=False
    )
```

```python
import functools
import math

import jax
import jax.numpy as jnp
from jax import lax
from jax.experimental import pallas as pl
from jax.experimental.pallas import tpu as pltpu
from jax.sharding import PartitionSpec as P

AXES = ("seq", "exp")
NT = (((1,), (1,)), ((), ()))
F32 = jnp.float32
BF16 = jnp.bfloat16
VMEM_LIMIT = 60 * 2**20
COST = 1000
PER_US = 1.15e9


def params():
    return pltpu.CompilerParams(vmem_limit_bytes=VMEM_LIMIT)


def inverse_rms(values):
    return 1.0 / jnp.sqrt(jnp.mean(values * values, axis=-1, keepdims=True) + 1e-06)


def send_kernel(images, patches, blocks, main, *refs):
    refs = refs[1:]
    levels = refs[:images]
    tokens_ref, cot_ref, routes_ref, codes_ref = refs[images : images + 4]
    outs = refs[images + 4 : images + 5 + blocks // 2]
    place_ref, normed_ref = refs[images + 5 + blocks // 2 :]
    rows = images * patches
    for image in range(images):
        part = slice(image * patches, (image + 1) * patches)
        level = levels[image][0].astype(F32)
        x = tokens_ref[part, :].astype(F32)
        pre = x * inverse_rms(x) * (1.0 + level[0:1]) + level[1:2]
        normed_ref[part, :] = pre.astype(BF16)
    routes = routes_ref[...]
    codes = codes_ref[...].astype(F32)
    weights = codes / jnp.sum(codes, axis=0, keepdims=True)
    expert = lax.broadcasted_iota(jnp.int32, (blocks, rows), 0)
    hot = jnp.zeros((blocks, rows), F32)
    share = jnp.zeros((blocks, rows), F32)
    for top in range(routes.shape[0]):
        match = routes[top : top + 1] == expert
        hot = hot + jnp.where(match, 1.0, 0.0)
        share = share + jnp.where(match, weights[top : top + 1], 0.0)
    before = lax.broadcasted_iota(jnp.int32, (rows, rows), 0) < lax.broadcasted_iota(
        jnp.int32, (rows, rows), 1
    )
    earlier = jnp.dot(
        hot.astype(BF16), jnp.where(before, 1.0, 0.0).astype(BF16), preferred_element_type=F32
    )
    place = jnp.where(hot > 0.0, earlier, -1.0)
    place_ref[...] = place
    slot = lax.broadcasted_iota(jnp.int32, (main + 8, rows), 0).astype(F32)
    span = 2 * main + 16
    for block in range(blocks):
        member = place[block : block + 1] == slot
        picked = jnp.where(member, 1.0, 0.0).astype(BF16)
        scale = jnp.sum(jnp.where(member, share[block : block + 1], 0.0), axis=1, keepdims=True)
        own = jnp.dot(picked, normed_ref[...], preferred_element_type=F32)
        grad = jnp.dot(picked, cot_ref[...], preferred_element_type=F32) * scale
        out = outs[block // 2] if block % 2 == 0 else outs[-1]
        start = 0 if block % 2 == 0 else block // 2 * span
        out[start : start + main, :] = own[0:main].astype(BF16)
        out[start + main : start + 2 * main, :] = grad[0:main].astype(BF16)
        out[start + 2 * main : start + span, :] = jnp.concatenate(
            [own[main:], grad[main:]], axis=0
        ).astype(BF16)


def level_specs(images, width):
    return [
        pl.BlockSpec((1, 2, width), lambda i, levels, image=image: (levels[image], 0, 0))
        for image in range(images)
    ]


def whole(shape):
    return pl.BlockSpec(shape, lambda i, levels: (0,) * len(shape))


def make_blocks(timesteps, modulation, tokens, cotangent, routes, codes, images, blocks, main):
    rows, width = tokens.shape
    half = blocks // 2
    shapes = [(2 * main + 16, width)] * half + [(half * (2 * main + 16), width)]
    return pl.pallas_call(
        functools.partial(send_kernel, images, rows // images, blocks, main),
        grid_spec=pltpu.PrefetchScalarGridSpec(
            num_scalar_prefetch=1,
            grid=(1,),
            in_specs=level_specs(images, width)
            + [whole(tokens.shape), whole(cotangent.shape), whole(routes.shape), whole(codes.shape)],
            out_specs=[whole(shape) for shape in shapes] + [whole((blocks, rows))],
            scratch_shapes=[pltpu.VMEM((rows, width), BF16)],
        ),
        out_shape=[jax.ShapeDtypeStruct(shape, BF16) for shape in shapes]
        + [jax.ShapeDtypeStruct((blocks, rows), F32)],
        compiler_params=params(),
        cost_estimate=pl.CostEstimate(flops=int(8 * PER_US), bytes_accessed=COST, transcendentals=0),
    )(timesteps, *([modulation] * images), tokens, cotangent, routes, codes)


def expert_kernel(pairs, sets, main, bases, has_own, *refs):
    refs = list(refs)

    def take(count):
        taken = refs[:count]
        del refs[:count]
        return taken

    arrived = take(pairs)
    sources = take(3) if has_own else []
    for _ in range(sets - has_own):
        sources += take(3)
    base = take(bases)
    del refs[: len(refs) - 6 - pairs]
    outs = take(pairs)
    xs, gs, es, held, row_sem, weight_sem = refs
    span = 2 * main + 16
    row_copies = []
    for at in range(2 * pairs):
        start, origin = at // 2 * span + at % 2 * main, at % 2 * span
        for low, high, target in (
            (0, main, xs.at[start : start + main, :]),
            (main, 2 * main, gs.at[start : start + main, :]),
            (2 * main, span, es.at[at * 16 : (at + 1) * 16, :]),
        ):
            row_copies.append(
                pltpu.make_async_copy(
                    arrived[at // 2].at[origin + low : origin + high, :],
                    target,
                    row_sem.at[len(row_copies)],
                )
            )
            row_copies[-1].start()
    weight_copies = [
        pltpu.make_async_copy(sources[at], held[at], weight_sem.at[at]) for at in range(3 * sets)
    ]

    def ready(at):
        if at + 1 < 3 * sets:
            weight_copies[at + 1].start()
        weight_copies[at].wait()

    weight_copies[0].start()
    for copy in row_copies:
        copy.wait()
    extra = es[...].astype(F32)
    for pair in range(pairs):
        start = pair * span + 2 * main
        low = [extra[at * 16 : at * 16 + 8] for at in (2 * pair, 2 * pair + 1)]
        high = [extra[at * 16 + 8 : at * 16 + 16] for at in (2 * pair, 2 * pair + 1)]
        xs[start : start + 16, :] = jnp.concatenate(low, axis=0).astype(BF16)
        gs[start : start + 16, :] = jnp.concatenate(high, axis=0).astype(BF16)
    total = None
    if bases:
        total = jnp.concatenate([item[...].astype(F32) for item in base], axis=0)
    for at in range(sets):
        gate_w, up_w, down_w = held[3 * at : 3 * at + 3]
        ready(3 * at)
        gate = jnp.dot(xs[...], gate_w[...], preferred_element_type=F32)
        ready(3 * at + 1)
        up = jnp.dot(xs[...], up_w[...], preferred_element_type=F32)
        ready(3 * at + 2)
        hidden = lax.dot_general(gs[...], down_w[...], NT, preferred_element_type=F32)
        sigma = jax.nn.sigmoid(gate)
        part = hidden * sigma
        grad_gate = (part * up * (1.0 + gate * (1.0 - sigma))).astype(BF16)
        grad_up = (part * gate).astype(BF16)
        back = lax.dot_general(grad_gate, gate_w[...], NT, preferred_element_type=F32)
        back = back + lax.dot_general(grad_up, up_w[...], NT, preferred_element_type=F32)
        total = back if total is None else total + back
    for pair in range(pairs):
        outs[pair][...] = total[pair * span : (pair + 1) * span].astype(outs[pair].dtype)


def expert_part(pairs, own, others, main, bases=(), dtypes=None, after=()):
    count = len(pairs)
    has_own = 0 if own is None else 1
    sets = has_own + len(others)
    width = pairs[0].shape[1]
    hidden = own[0].shape[1] if has_own else others[0][0].shape[1]
    span = 2 * main + 16
    anywhere = pl.BlockSpec(memory_space=pl.ANY)
    inside = pl.BlockSpec(memory_space=pltpu.VMEM)
    weights = list(own or []) + [item for other in others for item in other]
    shapes = [(width, hidden), (width, hidden), (hidden, width)] * sets
    dtypes = dtypes or [F32] * count
    return pl.pallas_call(
        functools.partial(expert_kernel, count, sets, main, len(bases), has_own),
        in_specs=[anywhere] * (count + len(weights))
        + [inside] * len(bases)
        + [anywhere] * len(after),
        out_specs=[inside] * count,
        out_shape=[jax.ShapeDtypeStruct((span, width), dtype) for dtype in dtypes],
        scratch_shapes=[
            pltpu.VMEM((span * count, width), BF16),
            pltpu.VMEM((span * count, width), BF16),
            pltpu.VMEM((32 * count, width), BF16),
            [pltpu.VMEM(shape, BF16) for shape in shapes],
            pltpu.SemaphoreType.DMA((6 * count,)),
            pltpu.SemaphoreType.DMA((3 * sets,)),
        ],
        compiler_params=params(),
        cost_estimate=pl.CostEstimate(
            flops=int((4 + 5 * count * sets) * PER_US), bytes_accessed=COST, transcendentals=0
        ),
    )(*pairs, *weights, *bases, *after)


def finish_kernel(images, patches, blocks, main, *refs):
    refs = refs[1:]
    levels = refs[:images]
    tokens_ref, place_ref = refs[images : images + 2]
    backs = refs[images + 2 : images + 2 + blocks]
    out_ref = refs[images + 2 + blocks]
    rows = images * patches
    place = place_ref[...]
    if main % 128 == 0:
        slot = lax.broadcasted_iota(jnp.int32, (rows, main), 1).astype(F32)
        member = jnp.concatenate(
            [
                jnp.where(place[:, block : block + 1] == slot, 1.0, 0.0).astype(BF16)
                for block in range(blocks)
            ],
            axis=1,
        )
    else:
        lane = lax.broadcasted_iota(jnp.int32, (rows, blocks * main), 1)
        member = jnp.zeros((rows, blocks * main), F32)
        for block in range(blocks):
            slot = (lane - block * main).astype(F32)
            here = (lane >= block * main) & (lane < (block + 1) * main)
            member = jnp.where(here & (place[:, block : block + 1] == slot), 1.0, member)
        member = member.astype(BF16)
    lane = lax.broadcasted_iota(jnp.int32, (rows, 8 * blocks), 1)
    over = jnp.zeros((rows, 8 * blocks), F32)
    for block in range(blocks):
        slot = (lane - 8 * block + main).astype(F32)
        here = (lane >= 8 * block) & (lane < 8 * (block + 1))
        over = jnp.where(here & (place[:, block : block + 1] == slot), 1.0, over)
    grad = jnp.dot(
        member,
        jnp.concatenate([back[0:main, :] for back in backs], axis=0),
        preferred_element_type=F32,
    )
    tail = jnp.concatenate([back[main:, :].astype(F32) for back in backs], axis=0).astype(BF16)
    grad = grad + jnp.dot(over.astype(BF16), tail, preferred_element_type=F32)
    for image in range(images):
        part = slice(image * patches, (image + 1) * patches)
        level = levels[image][0].astype(F32)
        x = tokens_ref[part, :].astype(F32)
        scaled = grad[part] * (1.0 + level[0:1])
        inverse = inverse_rms(x)
        along = jnp.mean(scaled * x, axis=-1, keepdims=True) * (inverse * inverse)
        out_ref[part, :] = (inverse * (scaled - x * along)).astype(BF16)


def finish(timesteps, modulation, tokens, place, backs, images, main):
    rows, width = tokens.shape
    blocks = len(backs)
    return pl.pallas_call(
        functools.partial(finish_kernel, images, rows // images, blocks, main),
        grid_spec=pltpu.PrefetchScalarGridSpec(
            num_scalar_prefetch=1,
            grid=(1,),
            in_specs=level_specs(images, width)
            + [whole(tokens.shape), whole(place.shape)]
            + [whole(backs[0].shape)] * blocks,
            out_specs=whole(tokens.shape),
        ),
        out_shape=jax.ShapeDtypeStruct((rows, width), BF16),
        compiler_params=params(),
    )(timesteps, *([modulation] * images), tokens, place, *backs)


def per_device(
    tokens,
    timesteps,
    modulation,
    routes,
    gate_codes,
    gate_weight,
    up_weight,
    down_weight,
    cotangent,
):
    images, patches, width = tokens.shape
    top = routes.shape[3]
    rows = images * patches
    n_exp, n_seq = lax.axis_size("exp"), lax.axis_size("seq")
    blocks = n_exp * gate_weight.shape[0]
    capacity = top * rows // blocks + 1
    main = capacity - 1 if (capacity - 1) % 16 == 0 else -(-capacity // 16) * 16
    inner = 2 ** (int(math.log2(n_seq)) // 2)
    outer = n_seq // inner

    def other(seq, exp, shift, first):
        along_inner = first if (exp % 2 == 0 or inner != outer) else not first
        return seq ^ shift if along_inner else seq ^ (shift * inner)

    def swap_seq(value, shift, first):
        pairs = [
            (seq * n_exp + exp, other(seq, exp, shift, first) * n_exp + exp)
            for seq in range(n_seq)
            for exp in range(n_exp)
        ]
        return lax.ppermute(value, AXES, pairs)

    def swap_exp(value, shift):
        return lax.ppermute(value, "exp", [(at, at ^ shift) for at in range(n_exp)])

    me = lax.axis_index("exp")
    flat_tokens = tokens.reshape(rows, width)
    flat_cot = cotangent.reshape(rows, width)
    turned = jnp.transpose(routes[0] ^ me, (2, 1, 0)).reshape(top, rows)
    codes = jnp.transpose(gate_codes, (2, 0, 1)).reshape(top, rows)
    made = make_blocks(
        timesteps, modulation, flat_tokens, flat_cot, turned, codes, images, blocks, main
    )
    half = blocks // 2
    near, cross, place = made[:half], made[half], made[half + 1]

    def behind(value, *earlier):
        return lax.optimization_barrier((value, earlier))[0]

    own = (gate_weight[0], up_weight[0], down_weight[0])
    others = [
        tuple(swap_seq(item, shift, True) for item in own) for shift in range(1, inner)
    ]

    crossed = swap_exp(cross, 1)
    span = 2 * main + 16
    arrived = {}

    def send(at, *earlier):
        rows_at = jnp.concatenate([near[at], crossed[at * span : (at + 1) * span]], axis=0)
        if earlier:
            rows_at = behind(rows_at, *earlier)
        arrived[at] = swap_exp(rows_at, 2 * at) if at else rows_at

    if half == 4 and outer == 2:
        steps = [
            ("own", [(0, 0)], [], []),
            ("own", [(3, 0)], [], []),
            ("own", [(1, 0)], [], []),
            ("others", [(0, 0), (3, 0), (1, 0)], [], []),
            ("all", [(0, 1)], [], []),
            ("all", [(3, 1), (2, 0)], [], []),
            ("all", [(2, 1), (1, 1)], [0], []),
        ]
        swap_after = {0: ["others", 2], 3: ["others", 2], 2: ["step", 3], 1: ["step", 4]}
        send_after = {1: 0}
        held_over = (3,)
    else:
        origins = range(outer)
        steps = [("all", [(at, origin) for origin in origins], [], []) for at in range(half)]
        swap_after = {at: [] for at in range(half)}
        send_after = {}
        held_over = ()

    rows_of, partial, parts, totals, backs, ran = {}, {}, {}, {}, {}, []

    def bring(at):
        after = swap_after[at]
        if not after:
            mine = arrived[at]
        elif after[0] == "step":
            mine = behind(arrived[at], ran[after[1]])
        else:
            mine = behind(arrived[at], ran[after[1]], *others[-1])
        for shift in range(1, outer):
            rows_of[at, shift] = swap_seq(mine, shift, False)

    def complete(at, *earlier):
        total = behind(parts[at, 0], *earlier) if earlier else parts[at, 0]
        for shift in range(1, outer):
            total = total + swap_seq(parts[at, shift], shift, False).astype(F32)
        totals[at] = total.astype(BF16)
        for core in range(2):
            back = jnp.concatenate(
                [
                    totals[at][core * main : (core + 1) * main],
                    totals[at][2 * main + 8 * core : 2 * main + 8 * core + 8],
                ],
                axis=0,
            )
            shift = 2 * at + core
            backs[shift] = swap_exp(back, shift) if shift else back

    for at in reversed(range(half)):
        if at not in send_after:
            send(at)
    for kind, items, ready, home in steps:
        for at in send_after:
            if at not in arrived and len(ran) > send_after[at]:
                send(at, ran[send_after[at]], others[-1][0])
        for at in arrived:
            rows_of[at, 0] = arrived[at]
        for at, origin in items:
            if (at, origin) not in rows_of:
                bring(at)
        bases = [partial[item] for item in items] if kind == "others" else []
        dtypes = [F32 if kind == "own" or item[1] == 0 else BF16 for item in items]
        results = expert_part(
            [rows_of[item] for item in items],
            None if kind == "others" else own,
            [] if kind == "own" else others,
            main,
            bases=bases,
            dtypes=dtypes,
            after=ran[-1:] + [totals[at] for at in ready] + [backs[at] for at in home],
        )
        ran.append(results[0])
        for item, result in zip(items, results):
            (partial if kind == "own" else parts)[item] = result
        for at in range(half):
            if at in totals or at in held_over:
                continue
            if all((at, origin) in parts for origin in range(outer)):
                complete(at)
    for at in held_over:
        complete(at, ran[-1])
    out = finish(
        timesteps, modulation, flat_tokens, place.T, [backs[at] for at in range(blocks)], images, main
    )
    return out.reshape(images, patches, width)


def solution(mesh):
    in_specs = (
        P("exp", "seq", None),
        P("exp"),
        P(),
        P("exp", "seq", None, None),
        P("exp", "seq", None),
        P("exp", None, "seq"),
        P("exp", None, "seq"),
        P("exp", "seq", None),
        P("exp", "seq", None),
    )
    out_specs = P("exp", "seq", None)
    return jax.shard_map(
        per_device, mesh=mesh, in_specs=in_specs, out_specs=out_specs, check_vma=False
    )
```
